256 devices in a mesh: pool: 64 (over y_lo, z, x), head: 4 (over y_hi, core).
Axes of the slice: x: 4, y: 4 (y_hi: 2, y_lo: 2; y = y_hi * 2 + y_lo), z: 8, core: 2. Of those that a mesh axis runs over, the one named last changes fastest.
Arguments:
- queries: bfloat16 [64, 8192], P('pool', 'head'), may hold values from -12 to 12
- new_kv: bfloat16 [64, 2, 1024], P('pool', None, 'head'), may hold values from -8 to 8
- cache_kv: bfloat16 [1024, 2, 8, 256, 128], P('pool', None, 'head'), may hold values from -6 to 6
- out_weight: bfloat16 [8192, 8192], P('head', 'pool'), may hold values from -0.0625 to 0.0625
- block_table: int32 [32, 32], replicated, may hold values from 0 to 1023, as said below
- home_slot: int32 [32], replicated, may hold values from 0 to 63, as said below
- block_counts: int32 [1024], replicated, may hold values from 1 to 256, as said below
- lengths: int32 [32], replicated, may hold values from 2 to 8192, as said below
Outputs:
- attn_out: float32 [32, 8192], P(None, ('pool', 'head'))
The draws below stay inside these ranges and needn't reach their ends.
Inputs may be any that keep to these rules, and one draw needn't show every extreme that they name: `block_table`: every one of the 1024 blocks appears exactly once in the table; block b is held by pool device b // 16. `home_slot`: the slots are distinct; slot s belongs to pool device s. A block's valid tokens are its first block_counts positions; each request's first block has 2 or more. lengths[r] is at most the sum of block_counts over request r's blocks, and equal to that sum for at least one request.
All inputs are finite; a program needn't handle non-finite values.
Results may differ from the reference program's by a relative error of at most 0.005.
Values may be sent and summed in bfloat16 or wider, within the bound.
A program may use at most 128 MiB of HBM per device.

```python
import math
import jax
import jax.numpy as jnp
from jax import lax

D = 8192
QH = 64
KVH = 8
HD = 128
BLK = 256
SLOTS = 1
BLK_DEV = 16
REQ = 32
BLOCKS = 1024
MAXB = 32
N_POOL = 64


def layout(key):
    block_list = jax.random.permutation(jax.random.fold_in(key, 101), BLOCKS).astype(jnp.int32)
    block_list = block_list.reshape(REQ, MAXB)
    slot_total = N_POOL * SLOTS
    middle = (jax.random.permutation(jax.random.fold_in(key, 102), slot_total - 2).astype(jnp.int32) + 1)[:REQ - 2]
    ends = jnp.array([0, slot_total - 1], dtype=jnp.int32)
    home_rows = jnp.concatenate([ends, middle])
    home_rows = jax.random.permutation(jax.random.fold_in(key, 109), home_rows).astype(jnp.int32)
    holder = jnp.arange(BLOCKS, dtype=jnp.int32) // BLK_DEV
    chance = jax.random.randint(jax.random.fold_in(key, 103), (BLOCKS,), 0, N_POOL, dtype=jnp.int32)
    partial_fill = jax.random.randint(jax.random.fold_in(key, 104), (BLOCKS,), 1, BLK + 1, dtype=jnp.int32)
    counts = jnp.where(chance <= holder, BLK, partial_fill).astype(jnp.int32)
    counts = counts.at[block_list[REQ - 1]].set(BLK)
    first_block = block_list[:, 0]
    counts = counts.at[first_block].set(jnp.maximum(counts[first_block], 2))
    counts = counts.at[block_list[0, 1]].set(1)
    counts = counts.at[block_list[0, 2]].set(BLK)
    totals = jnp.sum(counts[block_list], axis=1).astype(jnp.int32)
    trimmed = jax.random.randint(jax.random.fold_in(key, 105), (REQ,), 0, totals // 2 + 1, dtype=jnp.int32)
    request_ids = jnp.arange(REQ, dtype=jnp.int32)
    lengths = jnp.maximum(totals - trimmed, 2)
    lengths = jnp.where(request_ids == REQ - 1, totals, lengths)
    lengths = jnp.where(request_ids == REQ // 2, 2, lengths).astype(jnp.int32)
    return (block_list, home_rows, counts, lengths)


def draw_block_table(key, part):
    block_list, home_rows, counts, lengths = layout(key)
    return block_list


def draw_home_slot(key, part):
    block_list, home_rows, counts, lengths = layout(key)
    return home_rows


def draw_block_counts(key, part):
    block_list, home_rows, counts, lengths = layout(key)
    return counts


def draw_lengths(key, part):
    block_list, home_rows, counts, lengths = layout(key)
    return lengths


def draw_queries(key, part):
    key = jax.random.fold_in(key, 1)
    array_shape = (N_POOL * SLOTS, QH, HD)
    values = jnp.clip(2.5 * jax.random.normal(key, array_shape), -12.0, 12.0)
    return values.reshape(N_POOL * SLOTS, QH * HD).astype(jnp.bfloat16)


def draw_cache_kv(key, part):
    key = jax.random.fold_in(key, 2)
    array_shape = (BLOCKS, 2, KVH, BLK, HD)
    values = jnp.clip(jax.random.normal(key, array_shape), -6.0, 6.0)
    return values.astype(jnp.bfloat16)


def block_levels(key, dims, shards, smallest, top_value):
    def one(dim, shards_of):
        draws = jax.random.uniform(jax.random.fold_in(jax.random.fold_in(key, 6), dim), (shards_of,), jnp.float32, smallest / len(shards), top_value / len(shards))
        return jnp.repeat(jnp.exp(draws), dims[dim] // shards_of).reshape((-1,) + (1,) * (len(dims) - dim - 1))

    level = one(*shards[0])
    for cut in shards[1:]:
        level = level * one(*cut)
    return level


def noise(stream_key, extent, spread, bound, split=(), kind=jnp.bfloat16):
    level = block_levels(stream_key, extent, split, -0.22, 0.18) if split else 1.0
    entries = jax.random.normal(stream_key, extent, jnp.float32) * spread * level
    return jnp.minimum(jnp.maximum(entries, -bound), bound).astype(kind)


def setup_inputs(seed: int = 0) -> dict:
    keys = jax.random.split(jax.random.key(seed), 9)
    queries = draw_queries(jax.random.fold_in(keys[8], 71), 0)
    new_kv = noise(keys[1], (N_POOL * SLOTS, 2, KVH * HD), 2.0, 8.0, ((0, 64), (2, 4)))
    cache_kv = draw_cache_kv(jax.random.fold_in(keys[8], 71), 0)
    out_weight = noise(keys[3], (QH * HD, D), (QH * HD) ** -0.5, 0.0625, ((0, 4), (1, 64)))
    block_table = draw_block_table(jax.random.fold_in(keys[8], 71), 0)
    home_slot = draw_home_slot(jax.random.fold_in(keys[8], 71), 0)
    block_counts = draw_block_counts(jax.random.fold_in(keys[8], 71), 0)
    lengths = draw_lengths(jax.random.fold_in(keys[8], 71), 0)
    return dict(queries=queries, new_kv=new_kv, cache_kv=cache_kv, out_weight=out_weight, block_table=block_table, home_slot=home_slot, block_counts=block_counts, lengths=lengths)


def reference(queries, new_kv, cache_kv, out_weight, block_table, home_slot, block_counts, lengths):
    per_group = QH // KVH
    score_scale = 1.0 / math.sqrt(HD)
    positions = jnp.arange(BLK, dtype=jnp.int32)
    highest = lax.Precision.HIGHEST

    def attend_request(request):
        blocks = block_table[request]
        counts = block_counts[blocks]
        offsets = jnp.cumsum(counts) - counts
        live_mask = (positions[None, :] < counts[:, None]) & (offsets[:, None] + positions[None, :] < lengths[request])
        live_mask = live_mask.reshape(MAXB * BLK)
        cached = cache_kv[blocks].astype(jnp.float32)
        key_rows = jnp.transpose(cached[:, 0], (1, 0, 2, 3)).reshape(KVH, MAXB * BLK, HD)
        value_rows = jnp.transpose(cached[:, 1], (1, 0, 2, 3)).reshape(KVH, MAXB * BLK, HD)
        home_row = home_slot[request]
        query_heads = queries[home_row].astype(jnp.float32).reshape(KVH, per_group, HD)
        fresh_kv = new_kv[home_row].astype(jnp.float32).reshape(2, KVH, HD)
        scores = jnp.einsum('gjd,gtd->gjt', query_heads, key_rows, precision=highest) * score_scale
        scores = jnp.where(live_mask[None, None, :], scores, -jnp.inf)
        own_score = jnp.einsum('gjd,gd->gj', query_heads, fresh_kv[0], precision=highest) * score_scale
        top_score = jnp.maximum(lax.optimization_barrier(jnp.max(scores, axis=-1)), own_score)
        weights = jnp.exp(scores - top_score[..., None])
        own_weight = jnp.exp(own_score - top_score)
        total_weight = lax.optimization_barrier(jnp.sum(weights, axis=-1)) + own_weight
        rounded = weights.astype(jnp.bfloat16).astype(jnp.float32)
        own_rounded = own_weight.astype(jnp.bfloat16).astype(jnp.float32)
        mixed = jnp.einsum('gjt,gtd->gjd', rounded, value_rows, precision=highest)
        mixed = mixed + own_rounded[..., None] * fresh_kv[1][:, None, :]
        return (mixed / total_weight[..., None]).reshape(QH * HD).astype(jnp.bfloat16)
    attended = lax.map(attend_request, jnp.arange(REQ, dtype=jnp.int32))
    return jnp.dot(attended, out_weight, preferred_element_type=jnp.float32)
```

```python
import functools
import itertools
import math

import jax
import jax.numpy as jnp
from jax import lax
from jax.experimental import pallas as pl
from jax.experimental.pallas import tpu as pltpu
from jax.sharding import PartitionSpec as P

MESH = pl.DeviceIdType.MESH
LOW = -1e30
POOL = 64
HEADS = 4
Z, X = 8, 4
BLOCKS_HERE = 16
BLK = 256
HD = 128
REQ = 32
MAXB = 32
QH_HERE = 16
COMB = 32


def pool_offsets():
    steps = []
    for yl, z, x in itertools.product(range(2), range(Z), range(X)):
        hops = yl + min(z, Z - z) + min(x, X - x)
        if hops:
            steps.append((-hops, yl, z, x))
    return [step[1:] for step in sorted(steps)]


OFFSETS = pool_offsets()


def shifted(p, step):
    yl, z, x = p // 32, (p // X) % Z, p % X
    return ((yl + step[0]) % 2) * 32 + ((z + step[1]) % Z) * X + (x + step[2]) % X


def kernel(
    q_ref,
    new_ref,
    tab_v,
    tab_s,
    home_s,
    cnt_s,
    len_s,
    cache_hbm,
    w_hbm,
    out_ref,
    cache,
    weight,
    q_all,
    q_mine,
    scores,
    o_stack,
    o_send,
    o_recv,
    st_send,
    st_recv,
    st_turn,
    att_mine,
    att,
    y_all,
    load_sem,
    q_sem,
    p_sem,
    s_sem,
    a_sem,
    y_sem,
):
    p = lax.axis_index("pool")
    h = lax.axis_index("head")
    yl, z, x = p // 32, (p // X) % Z, p % X
    core = h % 2
    is_comb = (yl + z + x) % 2 == core
    mine = p // 2

    barrier = pltpu.get_barrier_semaphore()
    for step in OFFSETS:
        pl.semaphore_signal(
            barrier, inc=1, device_id=(shifted(p, step), h), device_id_type=MESH
        )
    for i in range(1, HEADS):
        pl.semaphore_signal(
            barrier, inc=1, device_id=(p, (h + i) % HEADS), device_id_type=MESH
        )
    loads = [
        pltpu.make_async_copy(cache_hbm.at[b], cache.at[b], load_sem.at[0])
        for b in range(BLOCKS_HERE)
    ]
    for load in loads:
        load.start()
    w_load = pltpu.make_async_copy(w_hbm, weight, load_sem.at[1])
    w_load.start()

    q_row = q_ref[...].astype(jnp.float32)
    q_rows = jnp.concatenate(
        [q_row[:, i * HD : (i + 1) * HD] for i in range(QH_HERE)], axis=0
    )
    q_mine[...] = q_rows.astype(jnp.bfloat16)
    pl.semaphore_wait(barrier, POOL - 1 + HEADS - 1)

    for step in OFFSETS:
        pltpu.make_async_remote_copy(
            q_mine,
            q_all.at[p],
            q_sem.at[0],
            q_sem.at[1],
            device_id=(shifted(p, step), h),
            device_id_type=MESH,
        ).start()
    pltpu.make_async_copy(q_mine, q_all.at[p], q_sem.at[1]).start()

    table = tab_v[...]
    entry = lax.broadcasted_iota(jnp.int32, (REQ, MAXB), 0) * MAXB + lax.broadcasted_iota(
        jnp.int32, (REQ, MAXB), 1
    )
    places = [
        jnp.max(jnp.where(table == p * BLOCKS_HERE + b, entry, 0))
        for b in range(BLOCKS_HERE)
    ]
    owners = [place >> 5 for place in places]
    ranks = [place & 31 for place in places]

    def add_counts(i, starts):
        return tuple(
            start + jnp.where(i < rank, cnt_s[tab_s[owner, i]], 0)
            for start, owner, rank in zip(starts, owners, ranks)
        )

    starts = lax.fori_loop(
        0, MAXB - 1, add_counts, tuple(jnp.int32(0) for _ in range(BLOCKS_HERE))
    )
    live = [
        jnp.minimum(cnt_s[p * BLOCKS_HERE + b], len_s[owners[b]] - starts[b])
        for b in range(BLOCKS_HERE)
    ]
    slots = [home_s[owner] for owner in owners]

    def find_own(r, found):
        return jnp.where(home_s[r] == p, r, found)

    own = lax.fori_loop(0, REQ, find_own, jnp.int32(2 * HD))

    scale = 1.0 / math.sqrt(HD)
    upper = lax.broadcasted_iota(jnp.int32, (QH_HERE, HD), 0) < 8
    new_kv = new_ref[0].astype(jnp.float32)
    new_k = jnp.where(upper, new_kv[0:1, :HD], new_kv[0:1, HD:])
    new_v = jnp.where(upper, new_kv[1:2, :HD], new_kv[1:2, HD:])
    own_score = jnp.sum(q_rows * new_k, axis=1, keepdims=True) * scale
    lane = lax.broadcasted_iota(jnp.int32, (QH_HERE, HD), 1)
    tops = jnp.where(lane == own, own_score, LOW)

    for load in loads:
        load.wait()
    whole = pltpu.make_async_copy(q_all, q_all, q_sem.at[1])
    whole.wait()
    token = lax.broadcasted_iota(jnp.int32, (QH_HERE, BLK), 1)
    for b in range(BLOCKS_HERE):
        q = q_all[slots[b]].astype(jnp.float32)
        wide = jnp.concatenate(
            [jnp.where(upper, q, 0.0), jnp.where(upper, 0.0, q)], axis=1
        ).astype(jnp.bfloat16)
        keys = jnp.concatenate([cache[b, 0, 0], cache[b, 0, 1]], axis=1)
        s = lax.dot_general(
            wide, keys, (((1,), (1,)), ((), ())), preferred_element_type=jnp.float32
        )
        s = jnp.where(token < live[b], s * scale, LOW)
        scores[b] = s
        top = jnp.max(s, axis=1, keepdims=True)
        tops = jnp.where(lane == owners[b], jnp.maximum(tops, top), tops)

    own_top = jnp.max(jnp.where(lane == own, tops, LOW), axis=1, keepdims=True)
    own_weight = jnp.exp(own_score - own_top)
    totals = jnp.where(lane == own, own_weight, 0.0)
    for b in range(BLOCKS_HERE):
        top = jnp.max(jnp.where(lane == owners[b], tops, LOW), axis=1, keepdims=True)
        weights = jnp.where(token < live[b], jnp.exp(scores[b] - top), 0.0)
        total = jnp.sum(weights, axis=1, keepdims=True)
        totals = jnp.where(lane == owners[b], totals + total, totals)
        values = jnp.concatenate([cache[b, 1, 0], cache[b, 1, 1]], axis=1)
        o = jnp.dot(
            weights.astype(jnp.bfloat16), values, preferred_element_type=jnp.float32
        )
        o = jnp.concatenate([o[:8, :HD], o[8:, HD:]], axis=0)
        o_stack[b * QH_HERE : (b + 1) * QH_HERE, :] = o.astype(jnp.bfloat16)

    stats = jnp.where(lane < REQ, totals, pltpu.roll(tops, REQ, 1))
    for i in range(QH_HERE):
        st_send[i] = stats[i : i + 1, :]

    column = lax.broadcasted_iota(jnp.int32, (1, BLOCKS_HERE * QH_HERE), 1)
    goal = jnp.zeros((1, BLOCKS_HERE * QH_HERE), jnp.int32)
    for b in range(BLOCKS_HERE):
        goal = jnp.where(column // QH_HERE == b, owners[b], goal)
    goal = goal + (column % QH_HERE) * REQ
    row = lax.broadcasted_iota(jnp.int32, (QH_HERE * REQ, BLOCKS_HERE * QH_HERE), 0)
    pick = jnp.where(row == goal, 1.0, 0.0).astype(jnp.bfloat16)
    merged = jnp.dot(pick, o_stack[...], preferred_element_type=jnp.float32)
    own_part = own_weight.astype(jnp.bfloat16).astype(jnp.float32) * new_v
    request = lax.broadcasted_iota(jnp.int32, (REQ, HD), 0)
    for i in range(QH_HERE):
        part = merged[i * REQ : (i + 1) * REQ, :]
        part = part + jnp.where(request == own, own_part[i : i + 1, :], 0.0)
        o_send[2 * i] = part[:16].astype(jnp.bfloat16)
        o_send[2 * i + 1] = part[16:].astype(jnp.bfloat16)

    for i in range(COMB):
        k = (mine + i + COMB // 2) % COMB
        to = 2 * k + (k // 16 + (k // 2) % Z + core) % 2

        def send(k=k, to=to):
            pltpu.make_async_remote_copy(
                st_send.at[k // 2],
                st_recv.at[p],
                s_sem.at[0],
                s_sem.at[1],
                device_id=(to, h),
                device_id_type=MESH,
            ).start()
            pltpu.make_async_remote_copy(
                o_send.at[k],
                o_recv.at[p],
                p_sem.at[0],
                p_sem.at[1],
                device_id=(to, h),
                device_id_type=MESH,
            ).start()

        if i == COMB // 2:

            @pl.when(is_comb)
            def _():
                pltpu.make_async_copy(
                    st_send.at[k // 2], st_recv.at[p], s_sem.at[1]
                ).start()
                pltpu.make_async_copy(o_send.at[k], o_recv.at[p], p_sem.at[1]).start()

            pl.when(jnp.logical_not(is_comb))(send)
        else:
            send()

    half = mine % 2

    @pl.when(is_comb)
    def _():
        pltpu.make_async_copy(st_recv, st_recv, s_sem.at[1]).wait()
        st_turn[...] = jnp.transpose(st_recv[:, 0, :])
        tot = st_turn[pl.ds(pl.multiple_of(half * 16, 16), 16), :]
        top = st_turn[pl.ds(pl.multiple_of(REQ + half * 16, 16), 16), :]
        top = jnp.where(tot > 0.0, top, LOW)
        most = jnp.max(top, axis=1, keepdims=True)
        factor = jnp.where(tot > 0.0, jnp.exp(top - most), 0.0)
        factor = factor / jnp.sum(factor * tot, axis=1, keepdims=True)
        pltpu.make_async_copy(o_recv, o_recv, p_sem.at[1]).wait()
        sums = [jnp.zeros((16, HD), jnp.float32) for _ in range(4)]
        for i in range(POOL):
            sums[i % 4] = sums[i % 4] + factor[:, i : i + 1] * o_recv[i].astype(
                jnp.float32
            )
        att_mine[...] = ((sums[0] + sums[1]) + (sums[2] + sums[3])).astype(jnp.bfloat16)
        for step in OFFSETS:
            pltpu.make_async_remote_copy(
                att_mine,
                att.at[mine],
                a_sem.at[0],
                a_sem.at[1],
                device_id=(shifted(p, step), h),
                device_id_type=MESH,
            ).start()
        pltpu.make_async_copy(att_mine, att.at[mine], a_sem.at[1]).start()

    w_load.wait()
    pltpu.make_async_copy(att, att, a_sem.at[1]).wait()
    wide = jnp.concatenate(
        [
            jnp.concatenate([att[2 * i], att[2 * i + 1]], axis=0)
            for i in range(QH_HERE)
        ],
        axis=1,
    )
    y_all[h] = jnp.dot(wide, weight[...], preferred_element_type=jnp.float32)
    y_copies = []
    for i in range(1, HEADS):
        copy = pltpu.make_async_remote_copy(
            y_all.at[h],
            y_all.at[h],
            y_sem.at[0],
            y_sem.at[1],
            device_id=(p, (h + i) % HEADS),
            device_id_type=MESH,
        )
        copy.start()
        y_copies.append(copy)
    three = y_all.at[pl.ds(0, HEADS - 1)]
    pltpu.make_async_copy(three, three, y_sem.at[1]).wait()
    y = (y_all[0] + y_all[1]) + (y_all[2] + y_all[3])
    part = y[:, :32]
    for i in range(1, HEADS):
        part = jnp.where(h == i, y[:, i * 32 : (i + 1) * 32], part)
    out_ref[...] = part

    pltpu.make_async_copy(three, three, y_sem.at[0]).wait()
    others = q_all.at[pl.ds(0, POOL - 1)]
    pltpu.make_async_copy(others, others, q_sem.at[0]).wait()

    @pl.when(is_comb)
    def _():
        most_o = o_send.at[pl.ds(0, COMB - 1)]
        pltpu.make_async_copy(most_o, most_o, p_sem.at[0]).wait()
        most_s = st_recv.at[pl.ds(0, COMB - 1)]
        pltpu.make_async_copy(most_s, most_s, s_sem.at[0]).wait()
        pltpu.make_async_copy(others, others, a_sem.at[0]).wait()

    @pl.when(jnp.logical_not(is_comb))
    def _():
        pltpu.make_async_copy(o_send, o_send, p_sem.at[0]).wait()
        all_s = st_recv.at[pl.ds(0, COMB)]
        pltpu.make_async_copy(all_s, all_s, s_sem.at[0]).wait()


def per_device(
    queries, new_kv, cache_kv, out_weight, block_table, home_slot, block_counts, lengths
):
    vmem = pl.BlockSpec(memory_space=pltpu.VMEM)
    smem = pl.BlockSpec(memory_space=pltpu.SMEM)
    hbm = pl.BlockSpec(memory_space=pltpu.HBM)
    bf16, f32 = jnp.bfloat16, jnp.float32
    dma = pltpu.SemaphoreType.DMA((2,))
    return pl.pallas_call(
        kernel,
        out_shape=jax.ShapeDtypeStruct((REQ, 32), f32),
        in_specs=[vmem, vmem, vmem, smem, smem, smem, smem, hbm, hbm],
        out_specs=vmem,
        scratch_shapes=[
            pltpu.VMEM((BLOCKS_HERE, 2, 2, BLK, HD), bf16),
            pltpu.VMEM((QH_HERE * HD, HD), bf16),
            pltpu.VMEM((POOL, QH_HERE, HD), bf16),
            pltpu.VMEM((QH_HERE, HD), bf16),
            pltpu.VMEM((BLOCKS_HERE, QH_HERE, BLK), f32),
            pltpu.VMEM((BLOCKS_HERE * QH_HERE, HD), bf16),
            pltpu.VMEM((COMB, 16, HD), bf16),
            pltpu.VMEM((POOL, 16, HD), bf16),
            pltpu.VMEM((QH_HERE, 1, HD), f32),
            pltpu.VMEM((POOL, 1, HD), f32),
            pltpu.VMEM((HD, POOL), f32),
            pltpu.VMEM((16, HD), bf16),
            pltpu.VMEM((COMB, 16, HD), bf16),
            pltpu.VMEM((HEADS, REQ, HD), f32),
            dma,
            dma,
            dma,
            dma,
            dma,
            dma,
        ],
        compiler_params=pltpu.CompilerParams(
            collective_id=0, has_side_effects=True, vmem_limit_bytes=62 * 1024 * 1024
        ),
        name="decode",
    )(
        queries,
        new_kv,
        block_table,
        block_table,
        home_slot,
        block_counts,
        lengths,
        cache_kv,
        out_weight,
    )


def solution(mesh):
    return jax.shard_map(
        per_device,
        mesh=mesh,
        in_specs=(
            P("pool", "head"),
            P("pool", None, "head"),
            P("pool", None, "head", None, None),
            P("head", "pool"),
            P(),
            P(),
            P(),
            P(),
        ),
        out_specs=P(None, ("pool", "head")),
        check_vma=False,
    )
```

```python
import functools
import itertools
import math

import jax
import jax.numpy as jnp
from jax import lax
from jax.experimental import pallas as pl
from jax.experimental.pallas import tpu as pltpu
from jax.sharding import PartitionSpec as P

MESH = pl.DeviceIdType.MESH
LOW = -1e30
POOL = 64
HEADS = 4
Z, X = 8, 4
BLOCKS_HERE = 16
BLK = 256
HD = 128
REQ = 32
MAXB = 32
QH_HERE = 16
COMB = 32


def pool_offsets():
    steps = []
    for yl, z, x in itertools.product(range(2), range(Z), range(X)):
        hops = yl + min(z, Z - z) + min(x, X - x)
        if hops:
            steps.append((-hops, yl, z, x))
    return [step[1:] for step in sorted(steps)]


OFFSETS = pool_offsets()


def shifted(p, step):
    yl, z, x = p // 32, (p // X) % Z, p % X
    return ((yl + step[0]) % 2) * 32 + ((z + step[1]) % Z) * X + (x + step[2]) % X


def kernel(
    q_hbm,
    new_hbm,
    tab_hbm,
    home_hbm,
    cnt_hbm,
    len_hbm,
    cache_hbm,
    w_hbm,
    out_ref,
    q_ref,
    new_ref,
    tab_v,
    tab_s,
    home_s,
    cnt_s,
    len_s,
    cache,
    weight,
    q_all,
    q_mine,
    scores,
    o_stack,
    o_send,
    o_recv,
    st_send,
    st_recv,
    st_turn,
    att_mine,
    att,
    y_send,
    y_recv,
    load_sem,
    q_sem,
    p_sem,
    s_sem,
    a_sem,
    y_sem,
):
    p = lax.axis_index("pool")
    h = lax.axis_index("head")
    yl, z, x = p // 32, (p // X) % Z, p % X
    core = h % 2
    is_comb = (yl + z + x) % 2 == core
    mine = p // 2

    barrier = pltpu.get_barrier_semaphore()
    for step in OFFSETS:
        pl.semaphore_signal(
            barrier, inc=1, device_id=(shifted(p, step), h), device_id_type=MESH
        )
    for i in range(1, HEADS):
        pl.semaphore_signal(
            barrier, inc=1, device_id=(p, (h + i) % HEADS), device_id_type=MESH
        )
    q_load = pltpu.make_async_copy(q_hbm, q_ref, load_sem.at[2])
    q_load.start()
    small_loads = [
        pltpu.make_async_copy(source, target, load_sem.at[3 + i])
        for i, (source, target) in enumerate(
            (
                (tab_hbm, tab_v),
                (tab_hbm, tab_s),
                (cnt_hbm, cnt_s),
                (home_hbm, home_s),
                (len_hbm, len_s),
                (new_hbm, new_ref),
            )
        )
    ]
    for load in small_loads:
        load.start()
    loads = [
        pltpu.make_async_copy(cache_hbm.at[b], cache.at[b], load_sem.at[0])
        for b in range(BLOCKS_HERE)
    ]
    for load in loads:
        load.start()
    w_load = pltpu.make_async_copy(w_hbm, weight, load_sem.at[1])
    w_load.start()

    q_load.wait()
    q_row = q_ref[...].astype(jnp.float32)
    q_rows = jnp.concatenate(
        [q_row[:, i * HD : (i + 1) * HD] for i in range(QH_HERE)], axis=0
    )
    q_mine[...] = q_rows.astype(jnp.bfloat16)
    pl.semaphore_wait(barrier, POOL - 1 + HEADS - 1)

    for step in OFFSETS:
        pltpu.make_async_remote_copy(
            q_mine,
            q_all.at[p],
            q_sem.at[0],
            q_sem.at[1],
            device_id=(shifted(p, step), h),
            device_id_type=MESH,
        ).start()
    pltpu.make_async_copy(q_mine, q_all.at[p], q_sem.at[1]).start()

    for load in small_loads:
        load.wait()
    table = tab_v[...]
    entry = lax.broadcasted_iota(jnp.int32, (REQ, MAXB), 0) * MAXB + lax.broadcasted_iota(
        jnp.int32, (REQ, MAXB), 1
    )
    places = [
        jnp.max(jnp.where(table == p * BLOCKS_HERE + b, entry, 0))
        for b in range(BLOCKS_HERE)
    ]
    owners = [place >> 5 for place in places]
    ranks = [place & 31 for place in places]

    def add_counts(i, starts):
        return tuple(
            start + jnp.where(i < rank, cnt_s[tab_s[owner, i]], 0)
            for start, owner, rank in zip(starts, owners, ranks)
        )

    starts = lax.fori_loop(
        0, MAXB - 1, add_counts, tuple(jnp.int32(0) for _ in range(BLOCKS_HERE))
    )
    live = [
        jnp.minimum(cnt_s[p * BLOCKS_HERE + b], len_s[owners[b]] - starts[b])
        for b in range(BLOCKS_HERE)
    ]
    slots = [home_s[owner] for owner in owners]

    def find_own(r, found):
        return jnp.where(home_s[r] == p, r, found)

    own = lax.fori_loop(0, REQ, find_own, jnp.int32(2 * HD))

    scale = 1.0 / math.sqrt(HD)
    upper = lax.broadcasted_iota(jnp.int32, (QH_HERE, HD), 0) < 8
    new_kv = new_ref[0].astype(jnp.float32)
    new_k = jnp.where(upper, new_kv[0:1, :HD], new_kv[0:1, HD:])
    new_v = jnp.where(upper, new_kv[1:2, :HD], new_kv[1:2, HD:])
    own_score = jnp.sum(q_rows * new_k, axis=1, keepdims=True) * scale
    lane = lax.broadcasted_iota(jnp.int32, (QH_HERE, HD), 1)
    tops = jnp.where(lane == own, own_score, LOW)

    for load in loads:
        load.wait()
    whole = pltpu.make_async_copy(q_all, q_all, q_sem.at[1])
    whole.wait()
    token = lax.broadcasted_iota(jnp.int32, (QH_HERE, BLK), 1)
    for b in range(BLOCKS_HERE):
        q = q_all[slots[b]].astype(jnp.float32)
        wide = jnp.concatenate(
            [jnp.where(upper, q, 0.0), jnp.where(upper, 0.0, q)], axis=1
        ).astype(jnp.bfloat16)
        keys = jnp.concatenate([cache[b, 0, 0], cache[b, 0, 1]], axis=1)
        s = lax.dot_general(
            wide, keys, (((1,), (1,)), ((), ())), preferred_element_type=jnp.float32
        )
        s = jnp.where(token < live[b], s * scale, LOW)
        scores[b] = s
        top = jnp.max(s, axis=1, keepdims=True)
        tops = jnp.where(lane == owners[b], jnp.maximum(tops, top), tops)

    own_top = jnp.max(jnp.where(lane == own, tops, LOW), axis=1, keepdims=True)
    own_weight = jnp.exp(own_score - own_top)
    totals = jnp.where(lane == own, own_weight, 0.0)
    for b in range(BLOCKS_HERE):
        top = jnp.max(jnp.where(lane == owners[b], tops, LOW), axis=1, keepdims=True)
        weights = jnp.where(token < live[b], jnp.exp(scores[b] - top), 0.0)
        total = jnp.sum(weights, axis=1, keepdims=True)
        totals = jnp.where(lane == owners[b], totals + total, totals)
        values = jnp.concatenate([cache[b, 1, 0], cache[b, 1, 1]], axis=1)
        o = jnp.dot(
            weights.astype(jnp.bfloat16), values, preferred_element_type=jnp.float32
        )
        o = jnp.concatenate([o[:8, :HD], o[8:, HD:]], axis=0)
        o_stack[b * QH_HERE : (b + 1) * QH_HERE, :] = o.astype(jnp.bfloat16)

    stats = jnp.where(lane < REQ, totals, pltpu.roll(tops, REQ, 1))
    for i in range(QH_HERE):
        st_send[i] = stats[i : i + 1, :]

    column = lax.broadcasted_iota(jnp.int32, (1, BLOCKS_HERE * QH_HERE), 1)
    goal = jnp.zeros((1, BLOCKS_HERE * QH_HERE), jnp.int32)
    for b in range(BLOCKS_HERE):
        goal = jnp.where(column // QH_HERE == b, owners[b], goal)
    goal = goal + (column % QH_HERE) * REQ
    row = lax.broadcasted_iota(jnp.int32, (QH_HERE * REQ, BLOCKS_HERE * QH_HERE), 0)
    pick = jnp.where(row == goal, 1.0, 0.0).astype(jnp.bfloat16)
    merged = jnp.dot(pick, o_stack[...], preferred_element_type=jnp.float32)
    own_part = own_weight.astype(jnp.bfloat16).astype(jnp.float32) * new_v
    request = lax.broadcasted_iota(jnp.int32, (REQ, HD), 0)
    for i in range(QH_HERE):
        part = merged[i * REQ : (i + 1) * REQ, :]
        part = part + jnp.where(request == own, own_part[i : i + 1, :], 0.0)
        o_send[2 * i] = part[:16].astype(jnp.bfloat16)
        o_send[2 * i + 1] = part[16:].astype(jnp.bfloat16)

    for i in range(COMB):
        k = (mine + i + COMB // 2) % COMB
        to = 2 * k + (k // 16 + (k // 2) % Z + core) % 2

        def send(k=k, to=to):
            pltpu.make_async_remote_copy(
                st_send.at[k // 2],
                st_recv.at[p],
                s_sem.at[0],
                s_sem.at[1],
                device_id=(to, h),
                device_id_type=MESH,
            ).start()
            pltpu.make_async_remote_copy(
                o_send.at[k],
                o_recv.at[p],
                p_sem.at[0],
                p_sem.at[1],
                device_id=(to, h),
                device_id_type=MESH,
            ).start()

        if i == COMB // 2:

            @pl.when(is_comb)
            def _():
                pltpu.make_async_copy(
                    st_send.at[k // 2], st_recv.at[p], s_sem.at[1]
                ).start()
                pltpu.make_async_copy(o_send.at[k], o_recv.at[p], p_sem.at[1]).start()

            pl.when(jnp.logical_not(is_comb))(send)
        else:
            send()

    half = mine % 2

    @pl.when(is_comb)
    def _():
        pltpu.make_async_copy(st_recv, st_recv, s_sem.at[1]).wait()
        st_turn[...] = jnp.transpose(st_recv[:, 0, :])
        tot = st_turn[pl.ds(pl.multiple_of(half * 16, 16), 16), :]
        top = st_turn[pl.ds(pl.multiple_of(REQ + half * 16, 16), 16), :]
        top = jnp.where(tot > 0.0, top, LOW)
        most = jnp.max(top, axis=1, keepdims=True)
        factor = jnp.where(tot > 0.0, jnp.exp(top - most), 0.0)
        factor = factor / jnp.sum(factor * tot, axis=1, keepdims=True)
        pltpu.make_async_copy(o_recv, o_recv, p_sem.at[1]).wait()
        sums = [jnp.zeros((16, HD), jnp.float32) for _ in range(4)]
        for i in range(POOL):
            sums[i % 4] = sums[i % 4] + factor[:, i : i + 1] * o_recv[i].astype(
                jnp.float32
            )
        att_mine[...] = ((sums[0] + sums[1]) + (sums[2] + sums[3])).astype(jnp.bfloat16)
        for step in OFFSETS:
            pltpu.make_async_remote_copy(
                att_mine,
                att.at[mine],
                a_sem.at[0],
                a_sem.at[1],
                device_id=(shifted(p, step), h),
                device_id_type=MESH,
            ).start()
        pltpu.make_async_copy(att_mine, att.at[mine], a_sem.at[1]).start()

    w_load.wait()
    pltpu.make_async_copy(att, att, a_sem.at[1]).wait()
    wide = jnp.concatenate(
        [
            jnp.concatenate([att[2 * i], att[2 * i + 1]], axis=0)
            for i in range(QH_HERE)
        ],
        axis=1,
    )
    y = jnp.dot(wide, weight[...], preferred_element_type=jnp.float32)
    for i in range(HEADS):
        y_send[i] = jnp.concatenate(
            [y[8 * j : 8 * j + 8, 32 * i : 32 * i + 32] for j in range(4)], axis=1
        )
    for i in range(1, HEADS):
        pltpu.make_async_remote_copy(
            y_send.at[(h + i) % HEADS],
            y_recv.at[h],
            y_sem.at[0],
            y_sem.at[1],
            device_id=(p, (h + i) % HEADS),
            device_id_type=MESH,
        ).start()
    pltpu.make_async_copy(y_send.at[h], y_recv.at[h], y_sem.at[1]).start()
    pltpu.make_async_copy(y_recv, y_recv, y_sem.at[1]).wait()
    y = (y_recv[0] + y_recv[1]) + (y_recv[2] + y_recv[3])
    for j in range(4):
        out_ref[8 * j : 8 * j + 8, :] = y[:, 32 * j : 32 * j + 32]

    three = y_send.at[pl.ds(0, HEADS - 1)]
    pltpu.make_async_copy(three, three, y_sem.at[0]).wait()
    others = q_all.at[pl.ds(0, POOL - 1)]
    pltpu.make_async_copy(others, others, q_sem.at[0]).wait()

    @pl.when(is_comb)
    def _():
        most_o = o_send.at[pl.ds(0, COMB - 1)]
        pltpu.make_async_copy(most_o, most_o, p_sem.at[0]).wait()
        most_s = st_recv.at[pl.ds(0, COMB - 1)]
        pltpu.make_async_copy(most_s, most_s, s_sem.at[0]).wait()
        pltpu.make_async_copy(others, others, a_sem.at[0]).wait()

    @pl.when(jnp.logical_not(is_comb))
    def _():
        pltpu.make_async_copy(o_send, o_send, p_sem.at[0]).wait()
        all_s = st_recv.at[pl.ds(0, COMB)]
        pltpu.make_async_copy(all_s, all_s, s_sem.at[0]).wait()


def per_device(
    queries, new_kv, cache_kv, out_weight, block_table, home_slot, block_counts, lengths
):
    vmem = pl.BlockSpec(memory_space=pltpu.VMEM)
    hbm = pl.BlockSpec(memory_space=pltpu.HBM)
    bf16, f32 = jnp.bfloat16, jnp.float32
    dma = pltpu.SemaphoreType.DMA((2,))
    return pl.pallas_call(
        kernel,
        out_shape=pltpu.VMEM((REQ, 32), f32),
        in_specs=[hbm] * 8,
        out_specs=vmem,
        scratch_shapes=[
            pltpu.VMEM(queries.shape, bf16),
            pltpu.VMEM(new_kv.shape, bf16),
            pltpu.VMEM(block_table.shape, jnp.int32),
            pltpu.SMEM(block_table.shape, jnp.int32),
            pltpu.SMEM(home_slot.shape, jnp.int32),
            pltpu.SMEM(block_counts.shape, jnp.int32),
            pltpu.SMEM(lengths.shape, jnp.int32),
            pltpu.VMEM((BLOCKS_HERE, 2, 2, BLK, HD), bf16),
            pltpu.VMEM((QH_HERE * HD, HD), bf16),
            pltpu.VMEM((POOL, QH_HERE, HD), bf16),
            pltpu.VMEM((QH_HERE, HD), bf16),
            pltpu.VMEM((BLOCKS_HERE, QH_HERE, BLK), f32),
            pltpu.VMEM((BLOCKS_HERE * QH_HERE, HD), bf16),
            pltpu.VMEM((COMB, 16, HD), bf16),
            pltpu.VMEM((POOL, 16, HD), bf16),
            pltpu.VMEM((QH_HERE, 1, HD), f32),
            pltpu.VMEM((POOL, 1, HD), f32),
            pltpu.VMEM((HD, POOL), f32),
            pltpu.VMEM((16, HD), bf16),
            pltpu.VMEM((COMB, 16, HD), bf16),
            pltpu.VMEM((HEADS, 8, HD), f32),
            pltpu.VMEM((HEADS, 8, HD), f32),
            pltpu.SemaphoreType.DMA((9,)),
            dma,
            dma,
            dma,
            dma,
            dma,
        ],
        compiler_params=pltpu.CompilerParams(
            collective_id=0, has_side_effects=True, vmem_limit_bytes=62 * 1024 * 1024
        ),
        name="decode",
    )(
        queries,
        new_kv,
        block_table,
        home_slot,
        block_counts,
        lengths,
        cache_kv,
        out_weight,
    )


def solution(mesh):
    return jax.shard_map(
        per_device,
        mesh=mesh,
        in_specs=(
            P("pool", "head"),
            P("pool", None, "head"),
            P("pool", None, "head", None, None),
            P("head", "pool"),
            P(),
            P(),
            P(),
            P(),
        ),
        out_specs=P(None, ("pool", "head")),
        check_vma=False,
    )
```

```python
import functools
import itertools
import math

import jax
import jax.numpy as jnp
from jax import lax
from jax.experimental import pallas as pl
from jax.experimental.pallas import tpu as pltpu
from jax.sharding import PartitionSpec as P

MESH = pl.DeviceIdType.MESH
LOW = -1e30
POOL = 64
HEADS = 4
Z, X = 8, 4
BLOCKS_HERE = 16
BLK = 256
HD = 128
REQ = 32
MAXB = 32
QH_HERE = 16
COMB = 32


def pool_offsets():
    steps = []
    for yl, z, x in itertools.product(range(2), range(Z), range(X)):
        hops = yl + min(z, Z - z) + min(x, X - x)
        if hops:
            steps.append((-hops, yl, z, x))
    return [step[1:] for step in sorted(steps)]


OFFSETS = pool_offsets()
RELAYED = (2, Z - 2)
ROW = {step: row for row, step in enumerate((2, 6, 0, 1, 3, 4, 5, 7))}


def shifted(p, step):
    yl, z, x = p // 32, (p // X) % Z, p % X
    return ((yl + step[0]) % 2) * 32 + ((z + step[1]) % Z) * X + (x + step[2]) % X


def kernel(
    q_hbm,
    new_hbm,
    tab_hbm,
    home_hbm,
    cnt_hbm,
    len_hbm,
    cache_hbm,
    w_hbm,
    out_ref,
    q_ref,
    new_ref,
    tab_v,
    tab_s,
    home_s,
    cnt_s,
    len_s,
    cache,
    weight,
    q_all,
    q_mine,
    scores,
    turned,
    o_stack,
    o_send,
    o_recv,
    st_send,
    st_recv,
    st_turn,
    att_mine,
    att,
    y_send,
    y_recv,
    load_sem,
    q_sem,
    p_sem,
    s_sem,
    a_sem,
    y_sem,
):
    p = lax.axis_index("pool")
    h = lax.axis_index("head")
    yl, z, x = p // 32, (p // X) % Z, p % X
    core = h % 2
    is_comb = (yl + z + x) % 2 == core
    mine = p // 2

    barrier = pltpu.get_barrier_semaphore()
    for step in OFFSETS:
        pl.semaphore_signal(
            barrier, inc=1, device_id=(shifted(p, step), h), device_id_type=MESH
        )
    for i in range(1, HEADS):
        pl.semaphore_signal(
            barrier, inc=1, device_id=(p, (h + i) % HEADS), device_id_type=MESH
        )
    q_load = pltpu.make_async_copy(q_hbm, q_ref, load_sem.at[2])
    q_load.start()
    small_loads = [
        pltpu.make_async_copy(source, target, load_sem.at[3 + i])
        for i, (source, target) in enumerate(
            (
                (tab_hbm, tab_v),
                (tab_hbm, tab_s),
                (cnt_hbm, cnt_s),
                (home_hbm, home_s),
                (len_hbm, len_s),
                (new_hbm, new_ref),
            )
        )
    ]
    for load in small_loads:
        load.start()
    loads = [
        pltpu.make_async_copy(cache_hbm.at[b], cache.at[b], load_sem.at[0])
        for b in range(BLOCKS_HERE)
    ]
    for load in loads:
        load.start()
    w_load = pltpu.make_async_copy(w_hbm, weight, load_sem.at[1])
    w_load.start()

    q_load.wait()
    q_row = q_ref[...].astype(jnp.float32)
    q_rows = jnp.concatenate(
        [q_row[:, i * HD : (i + 1) * HD] for i in range(QH_HERE)], axis=0
    )
    q_mine[...] = q_rows.astype(jnp.bfloat16)
    pl.semaphore_wait(barrier, POOL - 1 + HEADS - 1)

    column = yl * X + x
    for along in RELAYED:
        pltpu.make_async_remote_copy(
            q_mine,
            q_all.at[column * Z + ROW[Z - along]],
            q_sem.at[0],
            q_sem.at[2],
            device_id=(shifted(p, (0, along, 0)), h),
            device_id_type=MESH,
        ).start()
    for step in OFFSETS:
        if step[1] not in RELAYED:
            pltpu.make_async_remote_copy(
                q_mine,
                q_all.at[column * Z + ROW[(Z - step[1]) % Z]],
                q_sem.at[0],
                q_sem.at[1],
                device_id=(shifted(p, step), h),
                device_id_type=MESH,
            ).start()
    pltpu.make_async_copy(
        q_mine, q_all.at[column * Z + ROW[0]], q_sem.at[1]
    ).start()
    two = q_all.at[pl.ds(column * Z, 2)]
    pltpu.make_async_copy(two, two, q_sem.at[2]).wait()
    for step in OFFSETS:
        if step[1] == 0:
            pltpu.make_async_remote_copy(
                two,
                two,
                q_sem.at[0],
                q_sem.at[1],
                device_id=(shifted(p, step), h),
                device_id_type=MESH,
            ).start()

    for load in small_loads:
        load.wait()
    table = tab_v[...]
    entry = lax.broadcasted_iota(jnp.int32, (REQ, MAXB), 0) * MAXB + lax.broadcasted_iota(
        jnp.int32, (REQ, MAXB), 1
    )
    places = [
        jnp.max(jnp.where(table == p * BLOCKS_HERE + b, entry, 0))
        for b in range(BLOCKS_HERE)
    ]
    owners = [place >> 5 for place in places]
    ranks = [place & 31 for place in places]

    def add_counts(i, starts):
        return tuple(
            start + jnp.where(i < rank, cnt_s[tab_s[owner, i]], 0)
            for start, owner, rank in zip(starts, owners, ranks)
        )

    starts = lax.fori_loop(
        0, MAXB - 1, add_counts, tuple(jnp.int32(0) for _ in range(BLOCKS_HERE))
    )
    live = [
        jnp.minimum(cnt_s[p * BLOCKS_HERE + b], len_s[owners[b]] - starts[b])
        for b in range(BLOCKS_HERE)
    ]
    slots = []
    for owner in owners:
        slot = home_s[owner]
        away = ((slot >> 2) - z) & (Z - 1)
        row = jnp.int32(0)
        for step, place in ROW.items():
            row = jnp.where(away == step, place, row)
        slots.append(((slot >> 5) * X + (slot & (X - 1))) * Z + row)

    def find_own(r, found):
        return jnp.where(home_s[r] == p, r, found)

    own = lax.fori_loop(0, REQ, find_own, jnp.int32(2 * HD))

    scale = 1.0 / math.sqrt(HD)
    upper = lax.broadcasted_iota(jnp.int32, (QH_HERE, HD), 0) < 8
    new_kv = new_ref[0].astype(jnp.float32)
    new_k = jnp.where(upper, new_kv[0:1, :HD], new_kv[0:1, HD:])
    new_v = jnp.where(upper, new_kv[1:2, :HD], new_kv[1:2, HD:])
    own_score = jnp.sum(q_rows * new_k, axis=1, keepdims=True) * scale
    lane = lax.broadcasted_iota(jnp.int32, (QH_HERE, HD), 1)
    tops = jnp.where(lane == own, own_score, LOW)

    for load in loads:
        load.wait()
    for b in range(BLOCKS_HERE):
        for i in range(2):
            turned[b, i * HD : (i + 1) * HD, :] = jnp.transpose(cache[b, 0, i])
    most = q_all.at[pl.ds(0, POOL - 2)]
    whole = pltpu.make_async_copy(most, most, q_sem.at[1])
    whole.wait()
    token = lax.broadcasted_iota(jnp.int32, (QH_HERE, BLK), 1)
    first = jnp.where(upper, 1.0, 0.0).astype(jnp.bfloat16)
    second = jnp.where(upper, 0.0, 1.0).astype(jnp.bfloat16)
    for b in range(BLOCKS_HERE):
        q = q_all[slots[b]]
        wide = jnp.concatenate([q * first, q * second], axis=1)
        s = jnp.dot(wide, turned[b], preferred_element_type=jnp.float32)
        s = jnp.where(token < live[b], s * scale, LOW)
        scores[b] = s
        top = jnp.max(s, axis=1, keepdims=True)
        tops = jnp.where(lane == owners[b], jnp.maximum(tops, top), tops)

    own_top = jnp.max(jnp.where(lane == own, tops, LOW), axis=1, keepdims=True)
    own_weight = jnp.exp(own_score - own_top)
    totals = jnp.where(lane == own, own_weight, 0.0)
    for b in range(BLOCKS_HERE):
        top = jnp.max(jnp.where(lane == owners[b], tops, LOW), axis=1, keepdims=True)
        weights = jnp.where(token < live[b], jnp.exp(scores[b] - top), 0.0)
        total = jnp.sum(weights, axis=1, keepdims=True)
        totals = jnp.where(lane == owners[b], totals + total, totals)
        values = jnp.concatenate([cache[b, 1, 0], cache[b, 1, 1]], axis=1)
        o = jnp.dot(
            weights.astype(jnp.bfloat16), values, preferred_element_type=jnp.float32
        )
        o = jnp.concatenate([o[:8, :HD], o[8:, HD:]], axis=0)
        o_stack[b * QH_HERE : (b + 1) * QH_HERE, :] = o.astype(jnp.bfloat16)

    stats = jnp.where(lane < REQ, totals, pltpu.roll(tops, REQ, 1))
    for i in range(QH_HERE):
        st_send[i] = stats[i : i + 1, :]

    column = lax.broadcasted_iota(jnp.int32, (1, BLOCKS_HERE * QH_HERE), 1)
    goal = jnp.zeros((1, BLOCKS_HERE * QH_HERE), jnp.int32)
    for b in range(BLOCKS_HERE):
        goal = jnp.where(column // QH_HERE == b, owners[b], goal)
    goal = goal + (column % QH_HERE) * REQ
    row = lax.broadcasted_iota(jnp.int32, (QH_HERE * REQ, BLOCKS_HERE * QH_HERE), 0)
    pick = jnp.where(row == goal, 1.0, 0.0).astype(jnp.bfloat16)
    merged = jnp.dot(pick, o_stack[...], preferred_element_type=jnp.float32)
    own_part = own_weight.astype(jnp.bfloat16).astype(jnp.float32) * new_v
    request = lax.broadcasted_iota(jnp.int32, (REQ, HD), 0)
    for i in range(QH_HERE):
        part = merged[i * REQ : (i + 1) * REQ, :]
        part = part + jnp.where(request == own, own_part[i : i + 1, :], 0.0)
        o_send[2 * i] = part[:16].astype(jnp.bfloat16)
        o_send[2 * i + 1] = part[16:].astype(jnp.bfloat16)

    def send_partials(parity):
        for step in OFFSETS:
            if sum(step) % 2 == parity:
                to = shifted(p, step)
                k = to // 2
                pltpu.make_async_remote_copy(
                    st_send.at[k // 2],
                    st_recv.at[p],
                    s_sem.at[0],
                    s_sem.at[1],
                    device_id=(to, h),
                    device_id_type=MESH,
                ).start()
                pltpu.make_async_remote_copy(
                    o_send.at[k],
                    o_recv.at[p],
                    p_sem.at[0],
                    p_sem.at[1],
                    device_id=(to, h),
                    device_id_type=MESH,
                ).start()

    @pl.when(is_comb)
    def _():
        send_partials(0)
        pltpu.make_async_copy(st_send.at[mine // 2], st_recv.at[p], s_sem.at[1]).start()
        pltpu.make_async_copy(o_send.at[mine], o_recv.at[p], p_sem.at[1]).start()

    @pl.when(jnp.logical_not(is_comb))
    def _():
        send_partials(1)

    half = mine % 2

    @pl.when(is_comb)
    def _():
        pltpu.make_async_copy(st_recv, st_recv, s_sem.at[1]).wait()
        st_turn[...] = jnp.transpose(st_recv[:, 0, :])
        tot = st_turn[pl.ds(pl.multiple_of(half * 16, 16), 16), :]
        top = st_turn[pl.ds(pl.multiple_of(REQ + half * 16, 16), 16), :]
        top = jnp.where(tot > 0.0, top, LOW)
        most = jnp.max(top, axis=1, keepdims=True)
        factor = jnp.where(tot > 0.0, jnp.exp(top - most), 0.0)
        factor = factor / jnp.sum(factor * tot, axis=1, keepdims=True)
        pltpu.make_async_copy(o_recv, o_recv, p_sem.at[1]).wait()
        sums = [jnp.zeros((16, HD), jnp.float32) for _ in range(4)]
        for i in range(POOL):
            sums[i % 4] = sums[i % 4] + factor[:, i : i + 1] * o_recv[i].astype(
                jnp.float32
            )
        att_mine[...] = ((sums[0] + sums[1]) + (sums[2] + sums[3])).astype(jnp.bfloat16)
        for step in OFFSETS:
            pltpu.make_async_remote_copy(
                att_mine,
                att.at[mine],
                a_sem.at[0],
                a_sem.at[1],
                device_id=(shifted(p, step), h),
                device_id_type=MESH,
            ).start()
        pltpu.make_async_copy(att_mine, att.at[mine], a_sem.at[1]).start()

    w_load.wait()
    pltpu.make_async_copy(att, att, a_sem.at[1]).wait()
    wide = jnp.concatenate(
        [
            jnp.concatenate([att[2 * i], att[2 * i + 1]], axis=0)
            for i in range(QH_HERE)
        ],
        axis=1,
    )
    y = jnp.dot(wide, weight[...], preferred_element_type=jnp.float32)
    for i in range(HEADS):
        y_send[i] = jnp.concatenate(
            [y[8 * j : 8 * j + 8, 32 * i : 32 * i + 32] for j in range(4)], axis=1
        )
    for i in range(1, HEADS):
        pltpu.make_async_remote_copy(
            y_send.at[(h + i) % HEADS],
            y_recv.at[h],
            y_sem.at[0],
            y_sem.at[1],
            device_id=(p, (h + i) % HEADS),
            device_id_type=MESH,
        ).start()
    pltpu.make_async_copy(y_send.at[h], y_recv.at[h], y_sem.at[1]).start()
    pltpu.make_async_copy(y_recv, y_recv, y_sem.at[1]).wait()
    y = (y_recv[0] + y_recv[1]) + (y_recv[2] + y_recv[3])
    for j in range(4):
        out_ref[8 * j : 8 * j + 8, :] = y[:, 32 * j : 32 * j + 32]

    three = y_send.at[pl.ds(0, HEADS - 1)]
    pltpu.make_async_copy(three, three, y_sem.at[0]).wait()
    others = q_all.at[pl.ds(0, POOL - 1)]
    pltpu.make_async_copy(others, others, q_sem.at[0]).wait()

    @pl.when(is_comb)
    def _():
        most_o = o_send.at[pl.ds(0, COMB - 1)]
        pltpu.make_async_copy(most_o, most_o, p_sem.at[0]).wait()
        most_s = st_recv.at[pl.ds(0, COMB - 1)]
        pltpu.make_async_copy(most_s, most_s, s_sem.at[0]).wait()
        pltpu.make_async_copy(others, others, a_sem.at[0]).wait()

    @pl.when(jnp.logical_not(is_comb))
    def _():
        pltpu.make_async_copy(o_send, o_send, p_sem.at[0]).wait()
        all_s = st_recv.at[pl.ds(0, COMB)]
        pltpu.make_async_copy(all_s, all_s, s_sem.at[0]).wait()


def per_device(
    queries, new_kv, cache_kv, out_weight, block_table, home_slot, block_counts, lengths
):
    vmem = pl.BlockSpec(memory_space=pltpu.VMEM)
    hbm = pl.BlockSpec(memory_space=pltpu.HBM)
    bf16, f32 = jnp.bfloat16, jnp.float32
    dma = pltpu.SemaphoreType.DMA((2,))
    return pl.pallas_call(
        kernel,
        out_shape=pltpu.VMEM((REQ, 32), f32),
        in_specs=[hbm] * 8,
        out_specs=vmem,
        scratch_shapes=[
            pltpu.VMEM(queries.shape, bf16),
            pltpu.VMEM(new_kv.shape, bf16),
            pltpu.VMEM(block_table.shape, jnp.int32),
            pltpu.SMEM(block_table.shape, jnp.int32),
            pltpu.SMEM(home_slot.shape, jnp.int32),
            pltpu.SMEM(block_counts.shape, jnp.int32),
            pltpu.SMEM(lengths.shape, jnp.int32),
            pltpu.VMEM((BLOCKS_HERE, 2, 2, BLK, HD), bf16),
            pltpu.VMEM((QH_HERE * HD, HD), bf16),
            pltpu.VMEM((POOL, QH_HERE, HD), bf16),
            pltpu.VMEM((QH_HERE, HD), bf16),
            pltpu.VMEM((BLOCKS_HERE, QH_HERE, BLK), f32),
            pltpu.VMEM((BLOCKS_HERE, 2 * HD, BLK), bf16),
            pltpu.VMEM((BLOCKS_HERE * QH_HERE, HD), bf16),
            pltpu.VMEM((COMB, 16, HD), bf16),
            pltpu.VMEM((POOL, 16, HD), bf16),
            pltpu.VMEM((QH_HERE, 1, HD), f32),
            pltpu.VMEM((POOL, 1, HD), f32),
            pltpu.VMEM((HD, POOL), f32),
            pltpu.VMEM((16, HD), bf16),
            pltpu.VMEM((COMB, 16, HD), bf16),
            pltpu.VMEM((HEADS, 8, HD), f32),
            pltpu.VMEM((HEADS, 8, HD), f32),
            pltpu.SemaphoreType.DMA((9,)),
            pltpu.SemaphoreType.DMA((3,)),
            dma,
            dma,
            dma,
            dma,
        ],
        compiler_params=pltpu.CompilerParams(
            collective_id=0, has_side_effects=True, vmem_limit_bytes=62 * 1024 * 1024
        ),
        name="decode",
    )(
        queries,
        new_kv,
        block_table,
        home_slot,
        block_counts,
        lengths,
        cache_kv,
        out_weight,
    )


def solution(mesh):
    return jax.shard_map(
        per_device,
        mesh=mesh,
        in_specs=(
            P("pool", "head"),
            P("pool", None, "head"),
            P("pool", None, "head", None, None),
            P("head", "pool"),
            P(),
            P(),
            P(),
            P(),
        ),
        out_specs=P(None, ("pool", "head")),
        check_vma=False,
    )
```

```python
import functools
import itertools
import math

import jax
import jax.numpy as jnp
from jax import lax
from jax.experimental import pallas as pl
from jax.experimental.pallas import tpu as pltpu
from jax.sharding import PartitionSpec as P

MESH = pl.DeviceIdType.MESH
LOW = -1e30
POOL = 64
HEADS = 4
Z, X = 8, 4
BLOCKS_HERE = 16
BLK = 256
HD = 128
REQ = 32
MAXB = 32
QH_HERE = 16
COMB = 32


def pool_offsets():
    steps = []
    for yl, z, x in itertools.product(range(2), range(Z), range(X)):
        hops = yl + min(z, Z - z) + min(x, X - x)
        if hops:
            steps.append((-hops, yl, z, x))
    return [step[1:] for step in sorted(steps)]


OFFSETS = pool_offsets()
IN_PLANE = [step for step in OFFSETS if step[1] == 0]
NEAR = (2, 6, 1, 7)
FAR = (4, 3, 5)
ROW = {step: row for row, step in enumerate(NEAR + (0,) + FAR)}


def shifted(p, step):
    yl, z, x = p // 32, (p // X) % Z, p % X
    return ((yl + step[0]) % 2) * 32 + ((z + step[1]) % Z) * X + (x + step[2]) % X


def kernel(
    q_hbm,
    new_hbm,
    tab_hbm,
    home_hbm,
    cnt_hbm,
    len_hbm,
    cache_hbm,
    w_hbm,
    out_ref,
    q_ref,
    new_ref,
    tab_v,
    tab_s,
    home_s,
    cnt_s,
    len_s,
    cache,
    weight,
    q_all,
    scores,
    turned,
    o_stack,
    o_send,
    o_recv,
    st_send,
    st_recv,
    st_turn,
    att_mine,
    att,
    y_send,
    y_recv,
    load_sem,
    q_sem,
    p_sem,
    s_sem,
    a_sem,
    y_sem,
):
    p = lax.axis_index("pool")
    h = lax.axis_index("head")
    yl, z, x = p // 32, (p // X) % Z, p % X
    core = h % 2
    is_comb = (yl + z + x) % 2 == core
    mine = p // 2

    barrier = pltpu.get_barrier_semaphore()
    for step in [(0, along, 0) for along in FAR + NEAR] + IN_PLANE:
        pl.semaphore_signal(
            barrier, inc=1, device_id=(shifted(p, step), h), device_id_type=MESH
        )
    for i in range(1, HEADS):
        pl.semaphore_signal(
            barrier, inc=1, device_id=(p, (h + i) % HEADS), device_id_type=MESH
        )
    q_load = pltpu.make_async_copy(q_hbm, q_ref, load_sem.at[2])
    q_load.start()
    small_loads = [
        pltpu.make_async_copy(source, target, load_sem.at[3 + i])
        for i, (source, target) in enumerate(
            (
                (tab_hbm, tab_v),
                (tab_hbm, tab_s),
                (cnt_hbm, cnt_s),
                (home_hbm, home_s),
                (len_hbm, len_s),
                (new_hbm, new_ref),
            )
        )
    ]
    for load in small_loads:
        load.start()
    loads = [
        pltpu.make_async_copy(cache_hbm.at[b], cache.at[b], load_sem.at[0])
        for b in range(BLOCKS_HERE)
    ]
    for load in loads:
        load.start()
    w_load = pltpu.make_async_copy(w_hbm, weight, load_sem.at[1])
    w_load.start()

    q_load.wait()
    q_row = q_ref[...].astype(jnp.float32)
    q_rows = jnp.concatenate(
        [q_row[:, i * HD : (i + 1) * HD] for i in range(QH_HERE)], axis=0
    )
    column = yl * X + x
    q_mine = q_all.at[column * Z + ROW[0]]
    q_mine[...] = q_rows.astype(jnp.bfloat16)
    pl.semaphore_wait(barrier, Z - 1 + len(IN_PLANE) + HEADS - 1)

    for along in FAR + NEAR:
        pltpu.make_async_remote_copy(
            q_mine,
            q_all.at[column * Z + ROW[Z - along]],
            q_sem.at[0],
            q_sem.at[3 if along in FAR else 2],
            device_id=(shifted(p, (0, along, 0)), h),
            device_id_type=MESH,
        ).start()

    def hand_on(rows):
        for step in IN_PLANE:
            pltpu.make_async_remote_copy(
                rows,
                rows,
                q_sem.at[0],
                q_sem.at[1],
                device_id=(shifted(p, step), h),
                device_id_type=MESH,
            ).start()

    hand_on(q_mine)

    for load in small_loads:
        load.wait()
    table = tab_v[...]
    entry = lax.broadcasted_iota(jnp.int32, (REQ, MAXB), 0) * MAXB + lax.broadcasted_iota(
        jnp.int32, (REQ, MAXB), 1
    )
    places = [
        jnp.max(jnp.where(table == p * BLOCKS_HERE + b, entry, 0))
        for b in range(BLOCKS_HERE)
    ]
    owners = [place >> 5 for place in places]
    ranks = [place & 31 for place in places]

    def add_counts(i, starts):
        return tuple(
            start + jnp.where(i < rank, cnt_s[tab_s[owner, i]], 0)
            for start, owner, rank in zip(starts, owners, ranks)
        )

    starts = lax.fori_loop(
        0, MAXB - 1, add_counts, tuple(jnp.int32(0) for _ in range(BLOCKS_HERE))
    )
    live = [
        jnp.minimum(cnt_s[p * BLOCKS_HERE + b], len_s[owners[b]] - starts[b])
        for b in range(BLOCKS_HERE)
    ]
    slots = []
    for owner in owners:
        slot = home_s[owner]
        away = ((slot >> 2) - z) & (Z - 1)
        row = jnp.int32(0)
        for step, place in ROW.items():
            row = jnp.where(away == step, place, row)
        slots.append(((slot >> 5) * X + (slot & (X - 1))) * Z + row)

    def find_own(r, found):
        return jnp.where(home_s[r] == p, r, found)

    own = lax.fori_loop(0, REQ, find_own, jnp.int32(2 * HD))

    near = q_all.at[pl.ds(column * Z, len(NEAR))]
    pltpu.make_async_copy(near, near, q_sem.at[2]).wait()
    hand_on(near)
    far = q_all.at[pl.ds(column * Z + len(NEAR) + 1, len(FAR))]
    pltpu.make_async_copy(far, far, q_sem.at[3]).wait()
    hand_on(far)

    scale = 1.0 / math.sqrt(HD)
    upper = lax.broadcasted_iota(jnp.int32, (QH_HERE, HD), 0) < 8
    new_kv = new_ref[0].astype(jnp.float32)
    new_k = jnp.where(upper, new_kv[0:1, :HD], new_kv[0:1, HD:])
    new_v = jnp.where(upper, new_kv[1:2, :HD], new_kv[1:2, HD:])
    own_score = jnp.sum(q_rows * new_k, axis=1, keepdims=True) * scale
    lane = lax.broadcasted_iota(jnp.int32, (QH_HERE, HD), 1)
    tops = jnp.where(lane == own, own_score, LOW)

    for load in loads:
        load.wait()
    for b in range(BLOCKS_HERE):
        for i in range(2):
            turned[b, i * HD : (i + 1) * HD, :] = jnp.transpose(cache[b, 0, i])
    most = q_all.at[pl.ds(0, POOL - Z)]
    whole = pltpu.make_async_copy(most, most, q_sem.at[1])
    whole.wait()
    token = lax.broadcasted_iota(jnp.int32, (QH_HERE, BLK), 1)
    first = jnp.where(upper, 1.0, 0.0).astype(jnp.bfloat16)
    second = jnp.where(upper, 0.0, 1.0).astype(jnp.bfloat16)
    for b in range(BLOCKS_HERE):
        q = q_all[slots[b]]
        wide = jnp.concatenate([q * first, q * second], axis=1)
        s = jnp.dot(wide, turned[b], preferred_element_type=jnp.float32)
        s = jnp.where(token < live[b], s * scale, LOW)
        scores[b] = s
        top = jnp.max(s, axis=1, keepdims=True)
        tops = jnp.where(lane == owners[b], jnp.maximum(tops, top), tops)

    own_top = jnp.max(jnp.where(lane == own, tops, LOW), axis=1, keepdims=True)
    own_weight = jnp.exp(own_score - own_top)
    totals = jnp.where(lane == own, own_weight, 0.0)
    for b in range(BLOCKS_HERE):
        top = jnp.max(jnp.where(lane == owners[b], tops, LOW), axis=1, keepdims=True)
        weights = jnp.where(token < live[b], jnp.exp(scores[b] - top), 0.0)
        total = jnp.sum(weights, axis=1, keepdims=True)
        totals = jnp.where(lane == owners[b], totals + total, totals)
        values = jnp.concatenate([cache[b, 1, 0], cache[b, 1, 1]], axis=1)
        o = jnp.dot(
            weights.astype(jnp.bfloat16), values, preferred_element_type=jnp.float32
        )
        o = jnp.concatenate([o[:8, :HD], o[8:, HD:]], axis=0)
        o_stack[b * QH_HERE : (b + 1) * QH_HERE, :] = o.astype(jnp.bfloat16)

    stats = jnp.where(lane < REQ, totals, pltpu.roll(tops, REQ, 1))
    for i in range(QH_HERE):
        st_send[i] = stats[i : i + 1, :]

    column = lax.broadcasted_iota(jnp.int32, (1, BLOCKS_HERE * QH_HERE), 1)
    goal = jnp.zeros((1, BLOCKS_HERE * QH_HERE), jnp.int32)
    for b in range(BLOCKS_HERE):
        goal = jnp.where(column // QH_HERE == b, owners[b], goal)
    goal = goal + (column % QH_HERE) * REQ
    row = lax.broadcasted_iota(jnp.int32, (QH_HERE * REQ, BLOCKS_HERE * QH_HERE), 0)
    pick = jnp.where(row == goal, 1.0, 0.0).astype(jnp.bfloat16)
    merged = jnp.dot(pick, o_stack[...], preferred_element_type=jnp.float32)
    own_part = own_weight.astype(jnp.bfloat16).astype(jnp.float32) * new_v
    request = lax.broadcasted_iota(jnp.int32, (REQ, HD), 0)
    for i in range(QH_HERE):
        part = merged[i * REQ : (i + 1) * REQ, :]
        part = part + jnp.where(request == own, own_part[i : i + 1, :], 0.0)
        o_send[2 * i] = part[:16].astype(jnp.bfloat16)
        o_send[2 * i + 1] = part[16:].astype(jnp.bfloat16)

    def send_partials(parity):
        for step in OFFSETS:
            if sum(step) % 2 == parity:
                to = shifted(p, step)
                k = to // 2
                pltpu.make_async_remote_copy(
                    st_send.at[k // 2],
                    st_recv.at[p],
                    s_sem.at[0],
                    s_sem.at[1],
                    device_id=(to, h),
                    device_id_type=MESH,
                ).start()
                pltpu.make_async_remote_copy(
                    o_send.at[k],
                    o_recv.at[p],
                    p_sem.at[0],
                    p_sem.at[1],
                    device_id=(to, h),
                    device_id_type=MESH,
                ).start()

    @pl.when(is_comb)
    def _():
        send_partials(0)
        pltpu.make_async_copy(st_send.at[mine // 2], st_recv.at[p], s_sem.at[1]).start()
        pltpu.make_async_copy(o_send.at[mine], o_recv.at[p], p_sem.at[1]).start()

    @pl.when(jnp.logical_not(is_comb))
    def _():
        send_partials(1)

    half = mine % 2

    @pl.when(is_comb)
    def _():
        pltpu.make_async_copy(st_recv, st_recv, s_sem.at[1]).wait()
        st_turn[...] = jnp.transpose(st_recv[:, 0, :])
        tot = st_turn[pl.ds(pl.multiple_of(half * 16, 16), 16), :]
        top = st_turn[pl.ds(pl.multiple_of(REQ + half * 16, 16), 16), :]
        top = jnp.where(tot > 0.0, top, LOW)
        most = jnp.max(top, axis=1, keepdims=True)
        factor = jnp.where(tot > 0.0, jnp.exp(top - most), 0.0)
        factor = factor / jnp.sum(factor * tot, axis=1, keepdims=True)
        pltpu.make_async_copy(o_recv, o_recv, p_sem.at[1]).wait()
        sums = [jnp.zeros((16, HD), jnp.float32) for _ in range(4)]
        for i in range(POOL):
            sums[i % 4] = sums[i % 4] + factor[:, i : i + 1] * o_recv[i].astype(
                jnp.float32
            )
        att_mine[...] = ((sums[0] + sums[1]) + (sums[2] + sums[3])).astype(jnp.bfloat16)
        for step in OFFSETS:
            pltpu.make_async_remote_copy(
                att_mine,
                att.at[mine],
                a_sem.at[0],
                a_sem.at[1],
                device_id=(shifted(p, step), h),
                device_id_type=MESH,
            ).start()
        pltpu.make_async_copy(att_mine, att.at[mine], a_sem.at[1]).start()

    w_load.wait()
    pltpu.make_async_copy(att, att, a_sem.at[1]).wait()
    wide = jnp.concatenate(
        [
            jnp.concatenate([att[2 * i], att[2 * i + 1]], axis=0)
            for i in range(QH_HERE)
        ],
        axis=1,
    )
    y = jnp.dot(wide, weight[...], preferred_element_type=jnp.float32)
    for i in range(HEADS):
        y_send[i] = jnp.concatenate(
            [y[8 * j : 8 * j + 8, 32 * i : 32 * i + 32] for j in range(4)], axis=1
        )
    for i in (2, 3, 1):
        pltpu.make_async_remote_copy(
            y_send.at[(h + i) % HEADS],
            y_recv.at[h],
            y_sem.at[0],
            y_sem.at[1],
            device_id=(p, (h + i) % HEADS),
            device_id_type=MESH,
        ).start()
    pltpu.make_async_copy(y_send.at[h], y_recv.at[h], y_sem.at[1]).start()
    others = q_all.at[pl.ds(0, POOL - 1)]
    pltpu.make_async_copy(others, others, q_sem.at[0]).wait()

    @pl.when(is_comb)
    def _():
        most_o = o_send.at[pl.ds(0, COMB - 1)]
        pltpu.make_async_copy(most_o, most_o, p_sem.at[0]).wait()
        most_s = st_recv.at[pl.ds(0, COMB - 1)]
        pltpu.make_async_copy(most_s, most_s, s_sem.at[0]).wait()
        pltpu.make_async_copy(others, others, a_sem.at[0]).wait()

    @pl.when(jnp.logical_not(is_comb))
    def _():
        pltpu.make_async_copy(o_send, o_send, p_sem.at[0]).wait()
        all_s = st_recv.at[pl.ds(0, COMB)]
        pltpu.make_async_copy(all_s, all_s, s_sem.at[0]).wait()

    three = y_send.at[pl.ds(0, HEADS - 1)]
    pltpu.make_async_copy(three, three, y_sem.at[0]).wait()
    pltpu.make_async_copy(y_recv, y_recv, y_sem.at[1]).wait()
    y = (y_recv[0] + y_recv[1]) + (y_recv[2] + y_recv[3])
    for j in range(4):
        out_ref[8 * j : 8 * j + 8, :] = y[:, 32 * j : 32 * j + 32]


def per_device(
    queries, new_kv, cache_kv, out_weight, block_table, home_slot, block_counts, lengths
):
    vmem = pl.BlockSpec(memory_space=pltpu.VMEM)
    hbm = pl.BlockSpec(memory_space=pltpu.HBM)
    bf16, f32 = jnp.bfloat16, jnp.float32
    dma = pltpu.SemaphoreType.DMA((2,))
    return pl.pallas_call(
        kernel,
        out_shape=pltpu.VMEM((REQ, 32), f32),
        in_specs=[hbm] * 8,
        out_specs=vmem,
        scratch_shapes=[
            pltpu.VMEM(queries.shape, bf16),
            pltpu.VMEM(new_kv.shape, bf16),
            pltpu.VMEM(block_table.shape, jnp.int32),
            pltpu.SMEM(block_table.shape, jnp.int32),
            pltpu.SMEM(home_slot.shape, jnp.int32),
            pltpu.SMEM(block_counts.shape, jnp.int32),
            pltpu.SMEM(lengths.shape, jnp.int32),
            pltpu.VMEM((BLOCKS_HERE, 2, 2, BLK, HD), bf16),
            pltpu.VMEM((QH_HERE * HD, HD), bf16),
            pltpu.VMEM((POOL, QH_HERE, HD), bf16),
            pltpu.VMEM((BLOCKS_HERE, QH_HERE, BLK), f32),
            pltpu.VMEM((BLOCKS_HERE, 2 * HD, BLK), bf16),
            pltpu.VMEM((BLOCKS_HERE * QH_HERE, HD), bf16),
            pltpu.VMEM((COMB, 16, HD), bf16),
            pltpu.VMEM((POOL, 16, HD), bf16),
            pltpu.VMEM((QH_HERE, 1, HD), f32),
            pltpu.VMEM((POOL, 1, HD), f32),
            pltpu.VMEM((HD, POOL), f32),
            pltpu.VMEM((16, HD), bf16),
            pltpu.VMEM((COMB, 16, HD), bf16),
            pltpu.VMEM((HEADS, 8, HD), f32),
            pltpu.VMEM((HEADS, 8, HD), f32),
            pltpu.SemaphoreType.DMA((9,)),
            pltpu.SemaphoreType.DMA((4,)),
            dma,
            dma,
            dma,
            dma,
        ],
        compiler_params=pltpu.CompilerParams(
            collective_id=0, has_side_effects=True, vmem_limit_bytes=62 * 1024 * 1024
        ),
        name="decode",
    )(
        queries,
        new_kv,
        block_table,
        home_slot,
        block_counts,
        lengths,
        cache_kv,
        out_weight,
    )


def solution(mesh):
    return jax.shard_map(
        per_device,
        mesh=mesh,
        in_specs=(
            P("pool", "head"),
            P("pool", None, "head"),
            P("pool", None, "head", None, None),
            P("head", "pool"),
            P(),
            P(),
            P(),
            P(),
        ),
        out_specs=P(None, ("pool", "head")),
        check_vma=False,
    )
```

```python
import functools
import itertools
import math

import jax
import jax.numpy as jnp
from jax import lax
from jax.experimental import pallas as pl
from jax.experimental.pallas import tpu as pltpu
from jax.sharding import PartitionSpec as P

MESH = pl.DeviceIdType.MESH
LOW = -1e30
POOL = 64
HEADS = 4
Z, X = 8, 4
BLOCKS_HERE = 16
BLK = 256
HD = 128
REQ = 32
MAXB = 32
QH_HERE = 16
COMB = 32


def pool_offsets():
    steps = []
    for yl, z, x in itertools.product(range(2), range(Z), range(X)):
        hops = yl + min(z, Z - z) + min(x, X - x)
        if hops:
            steps.append((-hops, yl, z, x))
    return [step[1:] for step in sorted(steps)]


OFFSETS = pool_offsets()
IN_PLANE = [step for step in OFFSETS if step[1] == 0]
TIERS = ((0,), (1,), (2,), (3,), (7, 6, 5, 4))
NEAR = (2, 6, 1, 7)
FAR = (4, 3, 5)
ROW = {step: row for row, step in enumerate(NEAR + (0,) + FAR)}


def shifted(p, step):
    yl, z, x = p // 32, (p // X) % Z, p % X
    return ((yl + step[0]) % 2) * 32 + ((z + step[1]) % Z) * X + (x + step[2]) % X


def kernel(
    q_hbm,
    new_hbm,
    tab_hbm,
    home_hbm,
    cnt_hbm,
    len_hbm,
    cache_hbm,
    w_hbm,
    out_ref,
    q_ref,
    new_ref,
    tab_v,
    tab_s,
    home_s,
    cnt_s,
    len_s,
    cache,
    weight,
    q_all,
    scores,
    turned,
    o_stack,
    o_send,
    o_recv,
    st_send,
    st_recv,
    st_turn,
    att_mine,
    att,
    y_send,
    y_recv,
    load_sem,
    q_sem,
    p_sem,
    s_sem,
    a_sem,
    y_sem,
):
    p = lax.axis_index("pool")
    h = lax.axis_index("head")
    yl, z, x = p // 32, (p // X) % Z, p % X
    core = h % 2
    is_comb = (yl + z + x) % 2 == core
    mine = p // 2

    barrier = pltpu.get_barrier_semaphore()
    for step in [(0, along, 0) for along in FAR + NEAR] + IN_PLANE:
        pl.semaphore_signal(
            barrier, inc=1, device_id=(shifted(p, step), h), device_id_type=MESH
        )
    for i in range(1, HEADS):
        pl.semaphore_signal(
            barrier, inc=1, device_id=(p, (h + i) % HEADS), device_id_type=MESH
        )
    q_load = pltpu.make_async_copy(q_hbm, q_ref, load_sem.at[2])
    q_load.start()
    small_loads = [
        pltpu.make_async_copy(source, target, load_sem.at[3 + i])
        for i, (source, target) in enumerate(
            (
                (tab_hbm, tab_v),
                (tab_hbm, tab_s),
                (cnt_hbm, cnt_s),
                (home_hbm, home_s),
                (len_hbm, len_s),
                (new_hbm, new_ref),
            )
        )
    ]
    for load in small_loads:
        load.start()
    loads = [
        pltpu.make_async_copy(cache_hbm.at[b], cache.at[b], load_sem.at[0])
        for b in range(BLOCKS_HERE)
    ]
    for load in loads:
        load.start()
    w_load = pltpu.make_async_copy(w_hbm, weight, load_sem.at[1])
    w_load.start()

    q_load.wait()
    q_row = q_ref[...].astype(jnp.float32)
    q_rows = jnp.concatenate(
        [q_row[:, i * HD : (i + 1) * HD] for i in range(QH_HERE)], axis=0
    )
    column = yl * X + x
    q_mine = q_all.at[column * Z + ROW[0]]
    q_mine[...] = q_rows.astype(jnp.bfloat16)
    pl.semaphore_wait(barrier, Z - 1 + len(IN_PLANE) + HEADS - 1)

    for along in FAR + NEAR:
        pltpu.make_async_remote_copy(
            q_mine,
            q_all.at[column * Z + ROW[Z - along]],
            q_sem.at[0],
            q_sem.at[3 if along in FAR else 2],
            device_id=(shifted(p, (0, along, 0)), h),
            device_id_type=MESH,
        ).start()

    def hand_on(rows):
        for step in IN_PLANE:
            pltpu.make_async_remote_copy(
                rows,
                rows,
                q_sem.at[0],
                q_sem.at[1],
                device_id=(shifted(p, step), h),
                device_id_type=MESH,
            ).start()

    hand_on(q_mine)

    for load in small_loads:
        load.wait()
    table = tab_v[...]
    entry = lax.broadcasted_iota(jnp.int32, (REQ, MAXB), 0) * MAXB + lax.broadcasted_iota(
        jnp.int32, (REQ, MAXB), 1
    )
    places = [
        jnp.max(jnp.where(table == p * BLOCKS_HERE + b, entry, 0))
        for b in range(BLOCKS_HERE)
    ]
    owners = [place >> 5 for place in places]
    ranks = [place & 31 for place in places]

    def add_counts(i, starts):
        return tuple(
            start + jnp.where(i < rank, cnt_s[tab_s[owner, i]], 0)
            for start, owner, rank in zip(starts, owners, ranks)
        )

    starts = lax.fori_loop(
        0, MAXB - 1, add_counts, tuple(jnp.int32(0) for _ in range(BLOCKS_HERE))
    )
    live = [
        jnp.minimum(cnt_s[p * BLOCKS_HERE + b], len_s[owners[b]] - starts[b])
        for b in range(BLOCKS_HERE)
    ]
    slots = []
    for owner in owners:
        slot = home_s[owner]
        away = ((slot >> 2) - z) & (Z - 1)
        row = jnp.int32(0)
        for step, place in ROW.items():
            row = jnp.where(away == step, place, row)
        slots.append(((slot >> 5) * X + (slot & (X - 1))) * Z + row)

    def find_own(r, found):
        return jnp.where(home_s[r] == p, r, found)

    own = lax.fori_loop(0, REQ, find_own, jnp.int32(2 * HD))

    near = q_all.at[pl.ds(column * Z, len(NEAR))]
    pltpu.make_async_copy(near, near, q_sem.at[2]).wait()
    hand_on(near)
    far = q_all.at[pl.ds(column * Z + len(NEAR) + 1, len(FAR))]
    pltpu.make_async_copy(far, far, q_sem.at[3]).wait()
    hand_on(far)

    scale = 1.0 / math.sqrt(HD)
    upper = lax.broadcasted_iota(jnp.int32, (QH_HERE, HD), 0) < 8
    new_kv = new_ref[0].astype(jnp.float32)
    new_k = jnp.where(upper, new_kv[0:1, :HD], new_kv[0:1, HD:])
    new_v = jnp.where(upper, new_kv[1:2, :HD], new_kv[1:2, HD:])
    own_score = jnp.sum(q_rows * new_k, axis=1, keepdims=True) * scale
    lane = lax.broadcasted_iota(jnp.int32, (QH_HERE, HD), 1)
    tops = jnp.where(lane == own, own_score, LOW)

    for load in loads:
        load.wait()
    for b in range(BLOCKS_HERE):
        for i in range(2):
            turned[b, i * HD : (i + 1) * HD, :] = jnp.transpose(cache[b, 0, i])
    most = q_all.at[pl.ds(0, POOL - Z)]
    whole = pltpu.make_async_copy(most, most, q_sem.at[1])
    whole.wait()
    token = lax.broadcasted_iota(jnp.int32, (QH_HERE, BLK), 1)
    first = jnp.where(upper, 1.0, 0.0).astype(jnp.bfloat16)
    second = jnp.where(upper, 0.0, 1.0).astype(jnp.bfloat16)
    for b in range(BLOCKS_HERE):
        q = q_all[slots[b]]
        wide = jnp.concatenate([q * first, q * second], axis=1)
        s = jnp.dot(wide, turned[b], preferred_element_type=jnp.float32)
        s = jnp.where(token < live[b], s * scale, LOW)
        scores[b] = s
        top = jnp.max(s, axis=1, keepdims=True)
        tops = jnp.where(lane == owners[b], jnp.maximum(tops, top), tops)

    own_top = jnp.max(jnp.where(lane == own, tops, LOW), axis=1, keepdims=True)
    own_weight = jnp.exp(own_score - own_top)
    totals = jnp.where(lane == own, own_weight, 0.0)
    for b in range(BLOCKS_HERE):
        top = jnp.max(jnp.where(lane == owners[b], tops, LOW), axis=1, keepdims=True)
        weights = jnp.where(token < live[b], jnp.exp(scores[b] - top), 0.0)
        total = jnp.sum(weights, axis=1, keepdims=True)
        totals = jnp.where(lane == owners[b], totals + total, totals)
        values = jnp.concatenate([cache[b, 1, 0], cache[b, 1, 1]], axis=1)
        o = jnp.dot(
            weights.astype(jnp.bfloat16), values, preferred_element_type=jnp.float32
        )
        o = jnp.concatenate([o[:8, :HD], o[8:, HD:]], axis=0)
        o_stack[b * QH_HERE : (b + 1) * QH_HERE, :] = o.astype(jnp.bfloat16)

    stats = jnp.where(lane < REQ, totals, pltpu.roll(tops, REQ, 1))
    for i in range(QH_HERE):
        st_send[i] = stats[i : i + 1, :]

    column = lax.broadcasted_iota(jnp.int32, (1, BLOCKS_HERE * QH_HERE), 1)
    goal = jnp.zeros((1, BLOCKS_HERE * QH_HERE), jnp.int32)
    for b in range(BLOCKS_HERE):
        goal = jnp.where(column // QH_HERE == b, owners[b], goal)
    goal = goal + (column % QH_HERE) * REQ
    row = lax.broadcasted_iota(jnp.int32, (QH_HERE * REQ, BLOCKS_HERE * QH_HERE), 0)
    pick = jnp.where(row == goal, 1.0, 0.0).astype(jnp.bfloat16)
    merged = jnp.dot(pick, o_stack[...], preferred_element_type=jnp.float32)
    own_part = own_weight.astype(jnp.bfloat16).astype(jnp.float32) * new_v
    request = lax.broadcasted_iota(jnp.int32, (REQ, HD), 0)
    for i in range(QH_HERE):
        part = merged[i * REQ : (i + 1) * REQ, :]
        part = part + jnp.where(request == own, own_part[i : i + 1, :], 0.0)
        o_send[2 * i] = part[:16].astype(jnp.bfloat16)
        o_send[2 * i + 1] = part[16:].astype(jnp.bfloat16)

    def send_partials(parity):
        for step in OFFSETS:
            if sum(step) % 2 == parity:
                to = shifted(p, step)
                k = to // 2
                pltpu.make_async_remote_copy(
                    st_send.at[k // 2],
                    st_recv.at[p],
                    s_sem.at[0],
                    s_sem.at[1],
                    device_id=(to, h),
                    device_id_type=MESH,
                ).start()
                pltpu.make_async_remote_copy(
                    o_send.at[k],
                    o_recv.at[p],
                    p_sem.at[0],
                    p_sem.at[1],
                    device_id=(to, h),
                    device_id_type=MESH,
                ).start()

    @pl.when(is_comb)
    def _():
        send_partials(0)
        pltpu.make_async_copy(st_send.at[mine // 2], st_recv.at[p], s_sem.at[1]).start()
        pltpu.make_async_copy(o_send.at[mine], o_recv.at[p], p_sem.at[1]).start()

    @pl.when(jnp.logical_not(is_comb))
    def _():
        send_partials(1)

    half = mine % 2

    @pl.when(is_comb)
    def _():
        pltpu.make_async_copy(st_recv, st_recv, s_sem.at[1]).wait()
        st_turn[...] = jnp.transpose(st_recv[:, 0, :])
        tot = st_turn[pl.ds(pl.multiple_of(half * 16, 16), 16), :]
        top = st_turn[pl.ds(pl.multiple_of(REQ + half * 16, 16), 16), :]
        top = jnp.where(tot > 0.0, top, LOW)
        most = jnp.max(top, axis=1, keepdims=True)
        factor = jnp.where(tot > 0.0, jnp.exp(top - most), 0.0)
        factor = factor / jnp.sum(factor * tot, axis=1, keepdims=True)
        pltpu.make_async_copy(o_recv, o_recv, p_sem.at[1]).wait()
        sums = [jnp.zeros((16, HD), jnp.float32) for _ in range(4)]
        for i in range(POOL):
            sums[i % 4] = sums[i % 4] + factor[:, i : i + 1] * o_recv[i].astype(
                jnp.float32
            )
        att_mine[...] = ((sums[0] + sums[1]) + (sums[2] + sums[3])).astype(jnp.bfloat16)
        def send_att(step, there):
            to_yl, to_x = (yl + step[0]) % 2, (x + step[2]) % X
            pltpu.make_async_remote_copy(
                att_mine,
                att.at[mine],
                a_sem.at[0],
                a_sem.at[1],
                device_id=(to_yl * 32 + there * X + to_x, h),
                device_id_type=MESH,
            ).start()

        for tier in TIERS:
            for step in IN_PLANE:
                for there in tier:
                    send_att(step, there)
            for there in tier:
                pl.when(z != there)(functools.partial(send_att, (0, 0, 0), there))
        pltpu.make_async_copy(att_mine, att.at[mine], a_sem.at[1]).start()

    w_load.wait()
    pltpu.make_async_copy(att, att, a_sem.at[1]).wait()
    wide = jnp.concatenate(
        [
            jnp.concatenate([att[2 * i], att[2 * i + 1]], axis=0)
            for i in range(QH_HERE)
        ],
        axis=1,
    )
    y = jnp.dot(wide, weight[...], preferred_element_type=jnp.float32)
    for i in range(HEADS):
        y_send[i] = jnp.concatenate(
            [y[8 * j : 8 * j + 8, 32 * i : 32 * i + 32] for j in range(4)], axis=1
        )
    for i in (2, 3, 1):
        pltpu.make_async_remote_copy(
            y_send.at[(h + i) % HEADS],
            y_recv.at[h],
            y_sem.at[0],
            y_sem.at[1],
            device_id=(p, (h + i) % HEADS),
            device_id_type=MESH,
        ).start()
    pltpu.make_async_copy(y_send.at[h], y_recv.at[h], y_sem.at[1]).start()
    others = q_all.at[pl.ds(0, POOL - 1)]
    pltpu.make_async_copy(others, others, q_sem.at[0]).wait()

    @pl.when(is_comb)
    def _():
        most_o = o_send.at[pl.ds(0, COMB - 1)]
        pltpu.make_async_copy(most_o, most_o, p_sem.at[0]).wait()
        most_s = st_recv.at[pl.ds(0, COMB - 1)]
        pltpu.make_async_copy(most_s, most_s, s_sem.at[0]).wait()
        pltpu.make_async_copy(others, others, a_sem.at[0]).wait()

    @pl.when(jnp.logical_not(is_comb))
    def _():
        pltpu.make_async_copy(o_send, o_send, p_sem.at[0]).wait()
        all_s = st_recv.at[pl.ds(0, COMB)]
        pltpu.make_async_copy(all_s, all_s, s_sem.at[0]).wait()

    three = y_send.at[pl.ds(0, HEADS - 1)]
    pltpu.make_async_copy(three, three, y_sem.at[0]).wait()
    pltpu.make_async_copy(y_recv, y_recv, y_sem.at[1]).wait()
    y = (y_recv[0] + y_recv[1]) + (y_recv[2] + y_recv[3])
    for j in range(4):
        out_ref[8 * j : 8 * j + 8, :] = y[:, 32 * j : 32 * j + 32]


def per_device(
    queries, new_kv, cache_kv, out_weight, block_table, home_slot, block_counts, lengths
):
    vmem = pl.BlockSpec(memory_space=pltpu.VMEM)
    hbm = pl.BlockSpec(memory_space=pltpu.HBM)
    bf16, f32 = jnp.bfloat16, jnp.float32
    dma = pltpu.SemaphoreType.DMA((2,))
    return pl.pallas_call(
        kernel,
        out_shape=pltpu.VMEM((REQ, 32), f32),
        in_specs=[hbm] * 8,
        out_specs=vmem,
        scratch_shapes=[
            pltpu.VMEM(queries.shape, bf16),
            pltpu.VMEM(new_kv.shape, bf16),
            pltpu.VMEM(block_table.shape, jnp.int32),
            pltpu.SMEM(block_table.shape, jnp.int32),
            pltpu.SMEM(home_slot.shape, jnp.int32),
            pltpu.SMEM(block_counts.shape, jnp.int32),
            pltpu.SMEM(lengths.shape, jnp.int32),
            pltpu.VMEM((BLOCKS_HERE, 2, 2, BLK, HD), bf16),
            pltpu.VMEM((QH_HERE * HD, HD), bf16),
            pltpu.VMEM((POOL, QH_HERE, HD), bf16),
            pltpu.VMEM((BLOCKS_HERE, QH_HERE, BLK), f32),
            pltpu.VMEM((BLOCKS_HERE, 2 * HD, BLK), bf16),
            pltpu.VMEM((BLOCKS_HERE * QH_HERE, HD), bf16),
            pltpu.VMEM((COMB, 16, HD), bf16),
            pltpu.VMEM((POOL, 16, HD), bf16),
            pltpu.VMEM((QH_HERE, 1, HD), f32),
            pltpu.VMEM((POOL, 1, HD), f32),
            pltpu.VMEM((HD, POOL), f32),
            pltpu.VMEM((16, HD), bf16),
            pltpu.VMEM((COMB, 16, HD), bf16),
            pltpu.VMEM((HEADS, 8, HD), f32),
            pltpu.VMEM((HEADS, 8, HD), f32),
            pltpu.SemaphoreType.DMA((9,)),
            pltpu.SemaphoreType.DMA((4,)),
            dma,
            dma,
            dma,
            dma,
        ],
        compiler_params=pltpu.CompilerParams(
            collective_id=0, has_side_effects=True, vmem_limit_bytes=62 * 1024 * 1024
        ),
        name="decode",
    )(
        queries,
        new_kv,
        block_table,
        home_slot,
        block_counts,
        lengths,
        cache_kv,
        out_weight,
    )


def solution(mesh):
    return jax.shard_map(
        per_device,
        mesh=mesh,
        in_specs=(
            P("pool", "head"),
            P("pool", None, "head"),
            P("pool", None, "head", None, None),
            P("head", "pool"),
            P(),
            P(),
            P(),
            P(),
        ),
        out_specs=P(None, ("pool", "head")),
        check_vma=False,
    )
```
